512 devices in a mesh: rep: 8 (over x, core), shard: 64 (over z, y).
Axes of the slice: x: 4, y: 4, z: 16, core: 2. Of those that a mesh axis runs over, the one named last changes fastest.
Arguments:
- grad_partial: bfloat16 [8, 192, 262144], P('rep', None, 'shard'), may hold values from -6 to 6
- block_order: int32 [192], replicated, may hold values from 0 to 191, each once
- owner_slot: int32 [192], replicated, may hold values from 0 to 63, as said below
- left_root: bfloat16 [8, 64, 512, 512], P('rep', 'shard'), may hold values from -1 to 4, as said below
- right_root: bfloat16 [8, 64, 512, 512], P('rep', 'shard'), may hold values from -1 to 4, as said below
Outputs:
- left_gram: float32 [8, 64, 512, 512], P('rep', 'shard')
- right_gram: float32 [8, 64, 512, 512], P('rep', 'shard')
- update: bfloat16 [192, 262144], P('rep', 'shard')
The draws below stay inside these ranges and needn't reach their ends.
Inputs may be any that keep to these rules, and one draw needn't show every extreme that they name: `owner_slot`: entries g * 24 to (g + 1) * 24 - 1 are distinct for every group g. `left_root`: each matrix is symmetric. `right_root`: each matrix is symmetric.
All inputs are finite; a program needn't handle non-finite values.
Results may differ from the reference program's by a relative error of at most 0.02.
Values may be sent and summed in bfloat16 or wider, within the bound.
No kernel may reach another device: no remote copies, remote signals or barrier semaphores. Data moves between devices by JAX's collectives and lax.ppermute only.
A program may use at most 64 MiB of HBM per device.

```python
import math
import jax
import jax.numpy as jnp
from jax import lax

BLK = 512
NB = 192
SLOTS = 1
N_REP = 8
N_SHARD = 64


def assemble_root(offdiag, diagonal):
    unit = jnp.eye(BLK, dtype=jnp.float32)
    sym = 0.5 * (offdiag + jnp.swapaxes(offdiag, -1, -2))
    return sym * (1.0 - unit) + unit * diagonal[..., None]


def draw_owner_slot(key, part):
    key = jax.random.fold_in(key, 5)
    total = N_SHARD * SLOTS
    group_size = NB // N_REP
    group_keys = jax.random.split(key, N_REP)

    def one_group(group_key):
        first_key, second_key = jax.random.split(group_key)
        others = jax.random.permutation(first_key, total - 2) + 1
        values = jnp.concatenate([jnp.array([total - 1, 0], jnp.int32), others[:group_size - 2].astype(jnp.int32)])
        return values[jax.random.permutation(second_key, group_size)]
    return jax.vmap(one_group)(group_keys).reshape(NB).astype(jnp.int32)


def draw_left_root(key, part):
    key = jax.random.fold_in(key, 11)
    first_key, second_key = jax.random.split(key)
    shape = (N_REP, N_SHARD * SLOTS, BLK, BLK)
    offdiag = jax.random.normal(first_key, shape, jnp.float32) * (0.5 / math.sqrt(BLK))
    diagonal = jnp.exp(jax.random.uniform(second_key, shape[:-1], jnp.float32, math.log(0.3), math.log(3.0)))
    return assemble_root(offdiag, diagonal).astype(jnp.bfloat16)


def draw_right_root(key, part):
    key = jax.random.fold_in(key, 23)
    first_key, second_key = jax.random.split(key)
    shape = (N_REP, N_SHARD * SLOTS, BLK, BLK)
    offdiag = jax.random.normal(first_key, shape, jnp.float32) * (0.5 / math.sqrt(BLK))
    diagonal = jnp.exp(jax.random.uniform(second_key, shape[:-1], jnp.float32, math.log(0.3), math.log(3.0)))
    return assemble_root(offdiag, diagonal).astype(jnp.bfloat16)


def with_spikes(values, own_key, source, target, blocks, factor):
    def block_of(dim):
        return (jnp.arange(values.shape[dim]) // (values.shape[dim] // blocks)).reshape((-1,) + (1,) * (values.ndim - 1 - dim))

    near = jax.random.permutation(own_key, blocks)[block_of(target)]
    second = (block_of(target) + blocks // 2) % blocks
    return jnp.where((block_of(source) == near) | (block_of(source) == second), factor * values, values)


def level_of(stream_key, dims, shards, low, top_value):
    level, own = 1.0, jax.random.fold_in(stream_key, 6)
    for dim, blocks in shards:
        heights = jnp.exp(jax.random.uniform(jax.random.fold_in(own, dim), (blocks,), jnp.float32, low / len(shards), top_value / len(shards)))
        level = level * jnp.repeat(heights, dims[dim] // blocks).reshape([-1 if axis == dim else 1 for axis in range(len(dims))])
    return level


def noise_with(own_key, shape, width, most, cuts, heavy, kind=jnp.bfloat16):
    entries = width * jax.random.normal(own_key, shape, jnp.float32)
    if cuts:
        entries = entries * level_of(own_key, shape, cuts, -0.22, 0.18)
    return jnp.clip(with_spikes(entries, jax.random.fold_in(own_key, 3), *heavy), -most, most).astype(kind)


def setup_inputs(seed: int = 0) -> dict:
    arg_keys = jax.random.split(jax.random.key(seed), 6)
    grad_partial = noise_with(arg_keys[0], (N_REP, NB, BLK * BLK), 0.35, 6.0, ((0, 8), (2, 64)), (0, 1, 8, 2.0))
    block_order = jax.random.permutation(arg_keys[1], NB).astype(jnp.int32)
    owner_slot = draw_owner_slot(jax.random.fold_in(arg_keys[5], 71), 0)
    left_root = draw_left_root(jax.random.fold_in(arg_keys[5], 71), 0)
    right_root = draw_right_root(jax.random.fold_in(arg_keys[5], 71), 0)
    return dict(grad_partial=grad_partial, block_order=block_order, owner_slot=owner_slot, left_root=left_root, right_root=right_root)


graft_eps = 1e-06

def precondition(gradient, left_factor, right_factor):
    block_size = gradient.shape[0]
    left_stat = jnp.dot(gradient, gradient.T, preferred_element_type=jnp.float32) / block_size
    right_stat = jnp.dot(gradient.T, gradient, preferred_element_type=jnp.float32) / block_size
    half_product = jnp.dot(left_factor, gradient, preferred_element_type=jnp.float32).astype(jnp.bfloat16)
    shaped = jnp.dot(half_product, right_factor, preferred_element_type=jnp.float32)
    plain = gradient.astype(jnp.float32)
    graft_ratio = jnp.sqrt(jnp.mean(plain * plain) + graft_eps) / jnp.sqrt(jnp.mean(shaped * shaped) + graft_eps)
    return (left_stat, right_stat, (shaped * graft_ratio).astype(jnp.bfloat16))

def reference(grad_partial, block_order, owner_slot, left_root, right_root):
    group_size = NB // N_REP
    total_slots = N_SHARD * SLOTS

    def one_block(position):
        source = block_order[position]
        stacked = jnp.take(grad_partial, source, axis=1)
        gradient = lax.optimization_barrier(jnp.sum(stacked.astype(jnp.float32), axis=0)).astype(jnp.bfloat16).reshape(BLK, BLK)
        my_group = (position // group_size).astype(jnp.int32)
        target = owner_slot[position]
        return precondition(gradient, left_root[my_group, target], right_root[my_group, target])
    positions = jnp.arange(NB, dtype=jnp.int32)
    lefts, rights, updates = lax.map(one_block, positions)
    groups = (positions // group_size).astype(jnp.int32)
    zeros = jnp.zeros((N_REP, total_slots, BLK, BLK), jnp.float32)
    left_gram = zeros.at[groups, owner_slot].set(lefts)
    right_gram = zeros.at[groups, owner_slot].set(rights)
    update = updates.reshape(NB, BLK * BLK)
    return (left_gram, right_gram, update)
```

```python
import jax
import jax.numpy as jnp
from jax import lax
from jax.sharding import Mesh, PartitionSpec as P

graft_eps = 1e-06
rows = 8


def swap_core(value):
    return lax.ppermute(value, "core", [(0, 1), (1, 0)])


def per_device(grad_partial, block_order, owner_slot, left_root, right_root):
    x_count = lax.axis_size("x")
    shard_count = lax.axis_size("z") * lax.axis_size("y")
    my_shard = lax.axis_index(("z", "y"))
    my_core = lax.axis_index("core")
    my_group = lax.axis_index(("x", "core"))
    block_size = left_root.shape[2]
    block_count = grad_partial.shape[1]
    group_size = block_count // (2 * x_count)
    by_core = block_order.reshape(x_count, 2, group_size)
    partial = grad_partial[0].reshape(block_count, rows, block_size)
    kept_order = lax.dynamic_index_in_dim(by_core, my_core, 1, keepdims=False).reshape(-1)
    sent_order = lax.dynamic_index_in_dim(by_core, 1 - my_core, 1, keepdims=False).reshape(-1)
    kept = jnp.take(partial, kept_order, axis=0, mode="clip")
    sent = jnp.take(partial, sent_order, axis=0, mode="clip")
    chip = (kept.astype(jnp.float32) + swap_core(sent).astype(jnp.float32)).astype(jnp.bfloat16)
    chips = lax.all_to_all(chip, "x", 0, 0, tiled=True).reshape(
        x_count, group_size, rows, block_size
    )
    summed = jnp.sum(chips.astype(jnp.float32), axis=0).astype(jnp.bfloat16)

    owners = lax.dynamic_slice_in_dim(owner_slot, my_group * group_size, group_size)
    held = jnp.zeros((shard_count,), jnp.int32).at[owners].set(
        jnp.arange(group_size, dtype=jnp.int32)
    )
    owns = jnp.any(owners == my_shard)
    outgoing = jnp.take(summed, held, axis=0, mode="clip")
    received = lax.all_to_all(outgoing, ("z", "y"), 0, 0, tiled=True)
    block = jnp.where(owns, received.reshape(block_size, block_size), 0).astype(jnp.bfloat16)

    left_stat = (
        jnp.einsum("ab,cb->ac", block, block, preferred_element_type=jnp.float32) / block_size
    )
    right_stat = (
        jnp.einsum("ba,bc->ac", block, block, preferred_element_type=jnp.float32) / block_size
    )
    half_product = jnp.dot(left_root[0, 0], block, preferred_element_type=jnp.float32).astype(
        jnp.bfloat16
    )
    shaped = jnp.dot(half_product, right_root[0, 0], preferred_element_type=jnp.float32)
    plain = block.astype(jnp.float32)
    graft_ratio = jnp.sqrt(jnp.mean(plain * plain) + graft_eps) / jnp.sqrt(
        jnp.mean(shaped * shaped) + graft_eps
    )
    grafted = (shaped * graft_ratio).astype(jnp.bfloat16)
    returned = lax.all_to_all(
        grafted.reshape(shard_count, rows, block_size), ("z", "y"), 0, 0, tiled=True
    )
    update = jnp.take(returned, owners, axis=0, mode="clip").reshape(group_size, rows * block_size)
    return (left_stat[None, None], right_stat[None, None], update)


def solution(mesh):
    rep_count, shard_count = mesh.devices.shape
    split = Mesh(
        mesh.devices.reshape(rep_count // 2, 2, shard_count // 4, 4), ("x", "core", "z", "y")
    )
    return jax.shard_map(
        per_device,
        mesh=split,
        in_specs=(
            P(("x", "core"), None, ("z", "y")),
            P(),
            P(),
            P(("x", "core"), ("z", "y"), None, None),
            P(("x", "core"), ("z", "y"), None, None),
        ),
        out_specs=(
            P(("x", "core"), ("z", "y"), None, None),
            P(("x", "core"), ("z", "y"), None, None),
            P(("x", "core"), ("z", "y")),
        ),
        check_vma=False,
    )
```

```python
import jax
import jax.numpy as jnp
from jax import lax
from jax.experimental import pallas as pl
from jax.experimental.pallas import tpu as pltpu
from jax.sharding import Mesh, PartitionSpec as P

graft_eps = 1e-06
rows = 8


def swap_core(value):
    return lax.ppermute(value, "core", [(0, 1), (1, 0)])


def place_kernel(core, order, partial, sent_out, kept_out):
    group_size = order.shape[0] // 8
    for chip in range(4):
        for i in range(group_size):
            place = chip * group_size + i
            sent_out[place] = partial[order[(2 * chip + 1 - core[0]) * group_size + i]]
            kept_out[place] = partial[order[(2 * chip + core[0]) * group_size + i]]


def place(core, order, partial):
    smem = pl.BlockSpec(memory_space=pltpu.SMEM)
    vmem = pl.BlockSpec(memory_space=pltpu.VMEM)
    half = jax.ShapeDtypeStruct((partial.shape[0] // 2,) + partial.shape[1:], partial.dtype)
    return pl.pallas_call(
        place_kernel,
        out_shape=(half, half),
        in_specs=[smem, smem, vmem],
        out_specs=(vmem, vmem),
        compiler_params=pltpu.CompilerParams(vmem_limit_bytes=32 * 1024 * 1024),
        cost_estimate=pl.CostEstimate(
            flops=partial.size, bytes_accessed=4 * partial.size, transcendentals=0
        ),
    )(core, order, partial)


def slots_kernel(held, chips, outgoing, summed):
    for i in range(summed.shape[0]):
        total = chips[0, i].astype(jnp.float32)
        for x in range(1, chips.shape[0]):
            total += chips[x, i].astype(jnp.float32)
        summed[i] = total.astype(summed.dtype)
    for j in range(outgoing.shape[0]):
        outgoing[j] = summed[held[j]]


def slots(held, chips):
    vmem = pl.BlockSpec(memory_space=pltpu.VMEM)
    return pl.pallas_call(
        slots_kernel,
        out_shape=jax.ShapeDtypeStruct((held.shape[0],) + chips.shape[2:], chips.dtype),
        in_specs=[pl.BlockSpec(memory_space=pltpu.SMEM), vmem],
        out_specs=vmem,
        scratch_shapes=[pltpu.VMEM(chips.shape[1:], chips.dtype)],
        compiler_params=pltpu.CompilerParams(vmem_limit_bytes=32 * 1024 * 1024),
        cost_estimate=pl.CostEstimate(
            flops=chips.size, bytes_accessed=4 * chips.size, transcendentals=0
        ),
    )(held, chips)


def middle_kernel(owns, received, left, right, block_out, grafted_out):
    size = left.shape[0]
    block = jnp.where(owns[0] > 0, received[...].astype(jnp.float32), 0.0)
    plain = block.astype(jnp.bfloat16)
    block_out[...] = plain
    half = jnp.dot(left[...], plain, preferred_element_type=jnp.float32).astype(jnp.bfloat16)
    shaped = jnp.dot(half, right[...], preferred_element_type=jnp.float32)
    scale = 1.0 / (size * size)
    ratio = jnp.sqrt(jnp.sum(block * block, keepdims=True) * scale + graft_eps) / jnp.sqrt(
        jnp.sum(shaped * shaped, keepdims=True) * scale + graft_eps
    )
    grafted_out[...] = (shaped * ratio).astype(jnp.bfloat16)


def middle(owns, received, left, right):
    size = left.shape[0]
    vmem = pl.BlockSpec(memory_space=pltpu.VMEM)
    return pl.pallas_call(
        middle_kernel,
        out_shape=(jax.ShapeDtypeStruct((size, size), jnp.bfloat16),) * 2,
        in_specs=[pl.BlockSpec(memory_space=pltpu.SMEM)] + [vmem] * 3,
        out_specs=(vmem, vmem),
        compiler_params=pltpu.CompilerParams(vmem_limit_bytes=32 * 1024 * 1024),
        cost_estimate=pl.CostEstimate(
            flops=4 * size * size * size, bytes_accessed=10 * size * size, transcendentals=2
        ),
    )(owns, received, left, right)


def per_device(grad_partial, block_order, owner_slot, left_root, right_root):
    shard_count = lax.axis_size("z") * lax.axis_size("y")
    my_core = lax.axis_index("core")
    my_shard = lax.axis_index(("z", "y"))
    my_group = lax.axis_index(("x", "core"))
    block_size = left_root.shape[2]
    block_count = grad_partial.shape[1]
    group_size = block_count // (2 * lax.axis_size("x"))

    partial = grad_partial[0].reshape(block_count, rows, block_size)
    sent, kept = place(my_core[None].astype(jnp.int32), block_order, partial)
    chip = kept + swap_core(sent)
    chips = lax.all_to_all(chip, "x", 0, 0, tiled=True)
    chips = chips.reshape(-1, group_size, rows, block_size)

    owners = lax.dynamic_slice_in_dim(owner_slot, my_group * group_size, group_size)
    held = jnp.zeros((shard_count,), jnp.int32).at[owners].set(
        jnp.arange(group_size, dtype=jnp.int32)
    )
    owns = jnp.any(owners == my_shard).astype(jnp.int32)[None]
    outgoing = slots(held, chips)
    received = lax.all_to_all(outgoing, ("z", "y"), 0, 0, tiled=True)
    block, grafted = middle(
        owns, received.reshape(block_size, block_size), left_root[0, 0], right_root[0, 0]
    )
    returned = lax.all_to_all(
        grafted.reshape(shard_count, rows, block_size), ("z", "y"), 0, 0, tiled=True
    )
    update = jnp.take(returned, owners, axis=0, mode="clip").reshape(group_size, rows * block_size)
    left_stat = jnp.einsum("ab,cb->ac", block, block, preferred_element_type=jnp.float32)
    right_stat = jnp.einsum("ba,bc->ac", block, block, preferred_element_type=jnp.float32)
    return (left_stat[None, None] / block_size, right_stat[None, None] / block_size, update)


def solution(mesh):
    rep_count, shard_count = mesh.devices.shape
    split = Mesh(
        mesh.devices.reshape(rep_count // 2, 2, shard_count // 4, 4), ("x", "core", "z", "y")
    )
    return jax.shard_map(
        per_device,
        mesh=split,
        in_specs=(
            P(("x", "core"), None, ("z", "y")),
            P(),
            P(),
            P(("x", "core"), ("z", "y"), None, None),
            P(("x", "core"), ("z", "y"), None, None),
        ),
        out_specs=(
            P(("x", "core"), ("z", "y"), None, None),
            P(("x", "core"), ("z", "y"), None, None),
            P(("x", "core"), ("z", "y")),
        ),
        check_vma=False,
    )
```

```python
import jax
import jax.numpy as jnp
from jax import lax
from jax.experimental import pallas as pl
from jax.experimental.pallas import tpu as pltpu
from jax.sharding import Mesh, PartitionSpec as P

graft_eps = 1e-06
rows = 8


def swap_core(value):
    return lax.ppermute(value, "core", [(0, 1), (1, 0)])


def place_kernel(order, partial, sent_out, kept_out):
    core = lax.axis_index("core")
    group_size = order.shape[0] // 8
    for chip in range(4):
        for i in range(group_size):
            place = chip * group_size + i
            sent_out[place] = partial[order[(2 * chip + 1 - core) * group_size + i]]
            kept_out[place] = partial[order[(2 * chip + core) * group_size + i]]


def place(order, partial):
    smem = pl.BlockSpec(memory_space=pltpu.SMEM)
    vmem = pl.BlockSpec(memory_space=pltpu.VMEM)
    half = jax.ShapeDtypeStruct((partial.shape[0] // 2,) + partial.shape[1:], partial.dtype)
    return pl.pallas_call(
        place_kernel,
        out_shape=(half, half),
        in_specs=[smem, vmem],
        out_specs=(vmem, vmem),
        compiler_params=pltpu.CompilerParams(vmem_limit_bytes=32 * 1024 * 1024),
        cost_estimate=pl.CostEstimate(
            flops=partial.size, bytes_accessed=4 * partial.size, transcendentals=0
        ),
    )(order, partial)


def first_of_group(group_size):
    return lax.axis_index(("x", "core")) * group_size


def slots_kernel(owners, chips, outgoing):
    group_size = chips.shape[1]
    first = first_of_group(group_size)
    outgoing[...] = jnp.zeros_like(outgoing)
    for i in range(group_size):
        total = chips[0, i].astype(jnp.float32)
        for x in range(1, chips.shape[0]):
            total += chips[x, i].astype(jnp.float32)
        outgoing[owners[first + i]] = total.astype(jnp.bfloat16)


def slots(owners, chips, shard_count):
    vmem = pl.BlockSpec(memory_space=pltpu.VMEM)
    return pl.pallas_call(
        slots_kernel,
        out_shape=jax.ShapeDtypeStruct((shard_count,) + chips.shape[2:], chips.dtype),
        in_specs=[pl.BlockSpec(memory_space=pltpu.SMEM), vmem],
        out_specs=vmem,
        compiler_params=pltpu.CompilerParams(vmem_limit_bytes=32 * 1024 * 1024),
        cost_estimate=pl.CostEstimate(
            flops=chips.size, bytes_accessed=4 * chips.size, transcendentals=0
        ),
    )(owners, chips)


def middle_kernel(owns, received, left, right, block_out, grafted_out):
    size = left.shape[0]
    plain = jnp.where(owns[0] > 0, received[...], jnp.zeros_like(received))
    block_out[...] = plain
    block = plain.astype(jnp.float32)
    half = jnp.dot(left[...], plain, preferred_element_type=jnp.float32).astype(jnp.bfloat16)
    shaped = jnp.dot(half, right[...], preferred_element_type=jnp.float32)
    scale = 1.0 / (size * size)
    ratio = jnp.sqrt(jnp.sum(block * block, keepdims=True) * scale + graft_eps) / jnp.sqrt(
        jnp.sum(shaped * shaped, keepdims=True) * scale + graft_eps
    )
    grafted_out[...] = (shaped * ratio).astype(jnp.bfloat16)


def middle(owns, received, left, right):
    size = left.shape[0]
    vmem = pl.BlockSpec(memory_space=pltpu.VMEM)
    return pl.pallas_call(
        middle_kernel,
        out_shape=(jax.ShapeDtypeStruct((size, size), jnp.bfloat16),) * 2,
        in_specs=[pl.BlockSpec(memory_space=pltpu.SMEM)] + [vmem] * 3,
        out_specs=(vmem, vmem),
        compiler_params=pltpu.CompilerParams(vmem_limit_bytes=32 * 1024 * 1024),
        cost_estimate=pl.CostEstimate(
            flops=4 * size * size * size, bytes_accessed=10 * size * size, transcendentals=2
        ),
    )(owns, received, left, right)


def per_device(grad_partial, block_order, owner_slot, left_root, right_root):
    shard_count = lax.axis_size("z") * lax.axis_size("y")
    block_size = left_root.shape[2]
    group_size = grad_partial.shape[1] // (2 * lax.axis_size("x"))

    partial = grad_partial[0].reshape(-1, rows, block_size)
    sent, kept = place(block_order, partial)
    owners = lax.dynamic_slice_in_dim(owner_slot, first_of_group(group_size), group_size)
    owns = jnp.any(owners == lax.axis_index(("z", "y"))).astype(jnp.int32)[None]
    kept, owns = lax.optimization_barrier((kept, owns))
    chip = kept + swap_core(sent)
    chips = lax.all_to_all(chip, "x", 0, 0, tiled=True)
    outgoing = slots(owner_slot, chips.reshape(-1, group_size, rows, block_size), shard_count)
    received = lax.all_to_all(outgoing, ("z", "y"), 0, 0, tiled=True)
    block, grafted = middle(
        owns, received.reshape(block_size, block_size), left_root[0, 0], right_root[0, 0]
    )
    returned = lax.all_to_all(
        grafted.reshape(shard_count, rows, block_size), ("z", "y"), 0, 0, tiled=True
    )
    update = jnp.take(returned, owners, axis=0, mode="clip").reshape(group_size, -1)
    left_stat = jnp.einsum("ab,cb->ac", block, block, preferred_element_type=jnp.float32)
    right_stat = jnp.einsum("ba,bc->ac", block, block, preferred_element_type=jnp.float32)
    return (left_stat[None, None] / block_size, right_stat[None, None] / block_size, update)


def solution(mesh):
    rep_count, shard_count = mesh.devices.shape
    split = Mesh(
        mesh.devices.reshape(rep_count // 2, 2, shard_count // 4, 4), ("x", "core", "z", "y")
    )
    return jax.shard_map(
        per_device,
        mesh=split,
        in_specs=(
            P(("x", "core"), None, ("z", "y")),
            P(),
            P(),
            P(("x", "core"), ("z", "y"), None, None),
            P(("x", "core"), ("z", "y"), None, None),
        ),
        out_specs=(
            P(("x", "core"), ("z", "y"), None, None),
            P(("x", "core"), ("z", "y"), None, None),
            P(("x", "core"), ("z", "y")),
        ),
        check_vma=False,
    )
```

```python
import jax
import jax.numpy as jnp
from jax import lax
from jax.experimental import pallas as pl
from jax.experimental.pallas import tpu as pltpu
from jax.sharding import Mesh, PartitionSpec as P

graft_eps = 1e-06
rows = 8


def swap_core(value):
    return lax.ppermute(value, "core", [(0, 1), (1, 0)])


def place_kernel(order, partial, sent_out, kept_out):
    core = lax.axis_index("core")
    group_size = order.shape[0] // 8
    for chip in range(4):
        for i in range(group_size):
            place = chip * group_size + i
            sent_out[place] = partial[order[(2 * chip + 1 - core) * group_size + i]]
            kept_out[place] = partial[order[(2 * chip + core) * group_size + i]]


def place(order, partial):
    smem = pl.BlockSpec(memory_space=pltpu.SMEM)
    vmem = pl.BlockSpec(memory_space=pltpu.VMEM)
    half = jax.ShapeDtypeStruct((partial.shape[0] // 2,) + partial.shape[1:], partial.dtype)
    return pl.pallas_call(
        place_kernel,
        out_shape=(half, half),
        in_specs=[smem, vmem],
        out_specs=(vmem, vmem),
        compiler_params=pltpu.CompilerParams(vmem_limit_bytes=32 * 1024 * 1024),
        cost_estimate=pl.CostEstimate(
            flops=partial.size, bytes_accessed=4 * partial.size, transcendentals=0
        ),
    )(order, partial)


def first_of_group(group_size):
    return lax.axis_index(("x", "core")) * group_size


def slots_kernel(owners, *refs):
    parts, outgoing = refs[:-1], refs[-1]
    group_size = parts[0].shape[1]
    first = first_of_group(group_size)
    outgoing[...] = jnp.zeros_like(outgoing)
    for i in range(group_size):
        begin = 0
        for chips in parts:
            end = begin + chips.shape[3]
            total = chips[0, i].astype(jnp.float32)
            for x in range(1, chips.shape[0]):
                total += chips[x, i].astype(jnp.float32)
            outgoing[owners[first + i], :, begin:end] = total.astype(jnp.bfloat16)
            begin = end


def slots(owners, parts, shard_count):
    vmem = pl.BlockSpec(memory_space=pltpu.VMEM)
    size = sum(chips.size for chips in parts)
    width = sum(chips.shape[3] for chips in parts)
    return pl.pallas_call(
        slots_kernel,
        out_shape=jax.ShapeDtypeStruct((shard_count, rows, width), jnp.bfloat16),
        in_specs=[pl.BlockSpec(memory_space=pltpu.SMEM)] + [vmem] * len(parts),
        out_specs=vmem,
        compiler_params=pltpu.CompilerParams(vmem_limit_bytes=32 * 1024 * 1024),
        cost_estimate=pl.CostEstimate(flops=size, bytes_accessed=4 * size, transcendentals=0),
    )(owners, *parts)


def middle_kernel(owns, received, left, right, block_out, grafted_out):
    size = left.shape[0]
    plain = jnp.where(owns[0] > 0, received[...], jnp.zeros_like(received))
    block_out[...] = plain
    block = plain.astype(jnp.float32)
    half = jnp.dot(left[...], plain, preferred_element_type=jnp.float32).astype(jnp.bfloat16)
    shaped = jnp.dot(half, right[...], preferred_element_type=jnp.float32)
    scale = 1.0 / (size * size)
    ratio = jnp.sqrt(jnp.sum(block * block, keepdims=True) * scale + graft_eps) / jnp.sqrt(
        jnp.sum(shaped * shaped, keepdims=True) * scale + graft_eps
    )
    grafted_out[...] = (shaped * ratio).astype(jnp.bfloat16)


def middle(owns, received, left, right):
    size = left.shape[0]
    vmem = pl.BlockSpec(memory_space=pltpu.VMEM)
    return pl.pallas_call(
        middle_kernel,
        out_shape=(jax.ShapeDtypeStruct((size, size), jnp.bfloat16),) * 2,
        in_specs=[pl.BlockSpec(memory_space=pltpu.SMEM)] + [vmem] * 3,
        out_specs=(vmem, vmem),
        compiler_params=pltpu.CompilerParams(vmem_limit_bytes=32 * 1024 * 1024),
        cost_estimate=pl.CostEstimate(
            flops=4 * size * size * size, bytes_accessed=10 * size * size, transcendentals=2
        ),
    )(owns, received, left, right)


def per_device(grad_partial, block_order, owner_slot, left_root, right_root):
    shard_count = lax.axis_size("z") * lax.axis_size("y")
    block_size = left_root.shape[2]
    group_size = grad_partial.shape[1] // (2 * lax.axis_size("x"))

    partial = grad_partial[0].reshape(-1, rows, block_size)
    sent, kept = place(block_order, partial)
    owners = lax.dynamic_slice_in_dim(owner_slot, first_of_group(group_size), group_size)
    owns = jnp.any(owners == lax.axis_index(("z", "y"))).astype(jnp.int32)[None]
    kept, owns = lax.optimization_barrier((kept, owns))
    chip = kept + swap_core(sent)

    def chip_sums(shares):
        def exchange(chip):
            parts, begin = [], 0
            for share in shares:
                end = begin + share * block_size // sum(shares)
                part = lax.all_to_all(chip[:, :, begin:end], "x", 0, 0, tiled=True)
                parts.append(part.reshape(-1, group_size, rows, end - begin))
                begin = end
            return slots(owner_slot, parts, shard_count)

        return exchange

    at_once, in_turn = chip_sums((1,)), chip_sums((1, 3))
    outgoing = lax.cond(lax.axis_index("core") == 1, at_once, in_turn, chip)
    received = lax.all_to_all(outgoing, ("z", "y"), 0, 0, tiled=True)
    block, grafted = middle(
        owns, received.reshape(block_size, block_size), left_root[0, 0], right_root[0, 0]
    )
    returned = lax.all_to_all(
        grafted.reshape(shard_count, rows, block_size), ("z", "y"), 0, 0, tiled=True
    )
    update = jnp.take(returned, owners, axis=0, mode="clip").reshape(group_size, -1)
    left_stat = jnp.einsum("ab,cb->ac", block, block, preferred_element_type=jnp.float32)
    right_stat = jnp.einsum("ba,bc->ac", block, block, preferred_element_type=jnp.float32)
    return (left_stat[None, None] / block_size, right_stat[None, None] / block_size, update)


def solution(mesh):
    rep_count, shard_count = mesh.devices.shape
    split = Mesh(
        mesh.devices.reshape(rep_count // 2, 2, shard_count // 4, 4), ("x", "core", "z", "y")
    )
    return jax.shard_map(
        per_device,
        mesh=split,
        in_specs=(
            P(("x", "core"), None, ("z", "y")),
            P(),
            P(),
            P(("x", "core"), ("z", "y"), None, None),
            P(("x", "core"), ("z", "y"), None, None),
        ),
        out_specs=(
            P(("x", "core"), ("z", "y"), None, None),
            P(("x", "core"), ("z", "y"), None, None),
            P(("x", "core"), ("z", "y")),
        ),
        check_vma=False,
    )
```

```python
import jax
import jax.numpy as jnp
from jax import lax
from jax.experimental import pallas as pl
from jax.experimental.pallas import tpu as pltpu
from jax.sharding import Mesh, PartitionSpec as P

graft_eps = 1e-06
rows = 8


def swap_core(value):
    return lax.ppermute(value, "core", [(0, 1), (1, 0)])


def place_kernel(order, partial, sent_out, kept_out):
    core = lax.axis_index("core")
    group_size = order.shape[0] // 8
    for chip in range(4):
        for i in range(group_size):
            place = chip * group_size + i
            sent_out[place] = partial[order[(2 * chip + 1 - core) * group_size + i]]
            kept_out[place] = partial[order[(2 * chip + core) * group_size + i]]


def place(order, partial):
    smem = pl.BlockSpec(memory_space=pltpu.SMEM)
    vmem = pl.BlockSpec(memory_space=pltpu.VMEM)
    half = jax.ShapeDtypeStruct((partial.shape[0] // 2,) + partial.shape[1:], partial.dtype)
    return pl.pallas_call(
        place_kernel,
        out_shape=(half, half),
        in_specs=[smem, vmem],
        out_specs=(vmem, vmem),
        compiler_params=pltpu.CompilerParams(vmem_limit_bytes=32 * 1024 * 1024),
        cost_estimate=pl.CostEstimate(
            flops=partial.size, bytes_accessed=4 * partial.size, transcendentals=0
        ),
    )(order, partial)


def first_of_group(group_size):
    return lax.axis_index(("x", "core")) * group_size


def slots_kernel(owners, *refs):
    parts, outgoing = refs[:-1], refs[-1]
    first = first_of_group(sum(chips.shape[1] for chips in parts))
    outgoing[...] = jnp.zeros_like(outgoing)
    for chips in parts:
        for i in range(chips.shape[1]):
            total = chips[0, i].astype(jnp.float32)
            for x in range(1, chips.shape[0]):
                total += chips[x, i].astype(jnp.float32)
            outgoing[owners[first + i]] = total.astype(jnp.bfloat16)
        first += chips.shape[1]


def slots(owners, parts, shard_count):
    vmem = pl.BlockSpec(memory_space=pltpu.VMEM)
    size = sum(chips.size for chips in parts)
    return pl.pallas_call(
        slots_kernel,
        out_shape=jax.ShapeDtypeStruct((shard_count,) + parts[0].shape[2:], jnp.bfloat16),
        in_specs=[pl.BlockSpec(memory_space=pltpu.SMEM)] + [vmem] * len(parts),
        out_specs=vmem,
        compiler_params=pltpu.CompilerParams(vmem_limit_bytes=32 * 1024 * 1024),
        cost_estimate=pl.CostEstimate(flops=size, bytes_accessed=4 * size, transcendentals=0),
    )(owners, *parts)


def middle_kernel(owns, received, left, right, block_out, grafted_out):
    size = left.shape[0]
    plain = jnp.where(owns[0] > 0, received[...], jnp.zeros_like(received))
    block_out[...] = plain
    block = plain.astype(jnp.float32)
    half = jnp.dot(left[...], plain, preferred_element_type=jnp.float32).astype(jnp.bfloat16)
    shaped = jnp.dot(half, right[...], preferred_element_type=jnp.float32)
    scale = 1.0 / (size * size)
    ratio = jnp.sqrt(jnp.sum(block * block, keepdims=True) * scale + graft_eps) / jnp.sqrt(
        jnp.sum(shaped * shaped, keepdims=True) * scale + graft_eps
    )
    grafted_out[...] = (shaped * ratio).astype(jnp.bfloat16)


def middle(owns, received, left, right):
    size = left.shape[0]
    vmem = pl.BlockSpec(memory_space=pltpu.VMEM)
    return pl.pallas_call(
        middle_kernel,
        out_shape=(jax.ShapeDtypeStruct((size, size), jnp.bfloat16),) * 2,
        in_specs=[pl.BlockSpec(memory_space=pltpu.SMEM)] + [vmem] * 3,
        out_specs=(vmem, vmem),
        compiler_params=pltpu.CompilerParams(vmem_limit_bytes=32 * 1024 * 1024),
        cost_estimate=pl.CostEstimate(
            flops=4 * size * size * size, bytes_accessed=10 * size * size, transcendentals=2
        ),
    )(owns, received, left, right)


def per_device(grad_partial, block_order, owner_slot, left_root, right_root):
    shard_count = lax.axis_size("z") * lax.axis_size("y")
    block_size = left_root.shape[2]
    group_size = grad_partial.shape[1] // (2 * lax.axis_size("x"))

    partial = grad_partial[0].reshape(-1, rows, block_size)
    sent, kept = place(block_order, partial)
    owners = lax.dynamic_slice_in_dim(owner_slot, first_of_group(group_size), group_size)
    owns = jnp.any(owners == lax.axis_index(("z", "y"))).astype(jnp.int32)[None]
    kept, owns = lax.optimization_barrier((kept, owns))
    chip = kept + swap_core(sent)

    def chip_sums(counts):
        def exchange(chip):
            chip = chip.reshape(-1, group_size, rows, block_size)
            parts, begin = [], 0
            for count in counts:
                part = chip[:, begin : begin + count]
                parts.append(lax.all_to_all(part, "x", 0, 0, tiled=True))
                begin += count
            return slots(owner_slot, parts, shard_count)

        return exchange

    at_once, in_turn = chip_sums((group_size,)), chip_sums((2, group_size - 2))
    outgoing = lax.cond(lax.axis_index("core") == 1, at_once, in_turn, chip)
    received = lax.all_to_all(outgoing, ("z", "y"), 0, 0, tiled=True)
    block, grafted = middle(
        owns, received.reshape(block_size, block_size), left_root[0, 0], right_root[0, 0]
    )
    returned = lax.all_to_all(
        grafted.reshape(shard_count, rows, block_size), ("z", "y"), 0, 0, tiled=True
    )
    update = jnp.take(returned, owners, axis=0, mode="clip").reshape(group_size, -1)
    left_stat = jnp.einsum("ab,cb->ac", block, block, preferred_element_type=jnp.float32)
    right_stat = jnp.einsum("ba,bc->ac", block, block, preferred_element_type=jnp.float32)
    return (left_stat[None, None] / block_size, right_stat[None, None] / block_size, update)


def solution(mesh):
    rep_count, shard_count = mesh.devices.shape
    split = Mesh(
        mesh.devices.reshape(rep_count // 2, 2, shard_count // 4, 4), ("x", "core", "z", "y")
    )
    return jax.shard_map(
        per_device,
        mesh=split,
        in_specs=(
            P(("x", "core"), None, ("z", "y")),
            P(),
            P(),
            P(("x", "core"), ("z", "y"), None, None),
            P(("x", "core"), ("z", "y"), None, None),
        ),
        out_specs=(
            P(("x", "core"), ("z", "y"), None, None),
            P(("x", "core"), ("z", "y"), None, None),
            P(("x", "core"), ("z", "y")),
        ),
        check_vma=False,
    )
```

```python
import jax
import jax.numpy as jnp
from jax import lax
from jax.experimental import pallas as pl
from jax.experimental.pallas import tpu as pltpu
from jax.sharding import Mesh, PartitionSpec as P

graft_eps = 1e-06
rows = 8


def swap_core(value):
    return lax.ppermute(value, "core", [(0, 1), (1, 0)])


def place_kernel(order, partial, sent_out, kept_out):
    core = lax.axis_index("core")
    group_size = order.shape[0] // 8
    for chip in range(4):
        for i in range(group_size):
            place = chip * group_size + i
            sent_out[place] = partial[order[(2 * chip + 1 - core) * group_size + i]]
            kept_out[place] = partial[order[(2 * chip + core) * group_size + i]]


def place(order, partial):
    smem = pl.BlockSpec(memory_space=pltpu.SMEM)
    vmem = pl.BlockSpec(memory_space=pltpu.VMEM)
    half = jax.ShapeDtypeStruct((partial.shape[0] // 2,) + partial.shape[1:], partial.dtype)
    return pl.pallas_call(
        place_kernel,
        out_shape=(half, half),
        in_specs=[smem, vmem],
        out_specs=(vmem, vmem),
        compiler_params=pltpu.CompilerParams(vmem_limit_bytes=32 * 1024 * 1024),
        cost_estimate=pl.CostEstimate(
            flops=partial.size, bytes_accessed=4 * partial.size, transcendentals=0
        ),
    )(order, partial)


def first_of_group(group_size):
    return lax.axis_index(("x", "core")) * group_size


def slots_kernel(owners, *refs):
    parts, outgoing = refs[:-1], refs[-1]
    first = first_of_group(sum(chips.shape[1] for chips in parts))
    outgoing[...] = jnp.zeros_like(outgoing)
    for chips in parts:
        for i in range(chips.shape[1]):
            total = chips[0, i].astype(jnp.float32)
            for x in range(1, chips.shape[0]):
                total += chips[x, i].astype(jnp.float32)
            outgoing[owners[first + i]] = total.astype(jnp.bfloat16)
        first += chips.shape[1]


def slots(owners, parts, shard_count):
    vmem = pl.BlockSpec(memory_space=pltpu.VMEM)
    size = sum(chips.size for chips in parts)
    return pl.pallas_call(
        slots_kernel,
        out_shape=jax.ShapeDtypeStruct((shard_count,) + parts[0].shape[2:], jnp.bfloat16),
        in_specs=[pl.BlockSpec(memory_space=pltpu.SMEM)] + [vmem] * len(parts),
        out_specs=vmem,
        compiler_params=pltpu.CompilerParams(vmem_limit_bytes=32 * 1024 * 1024),
        cost_estimate=pl.CostEstimate(flops=size, bytes_accessed=4 * size, transcendentals=0),
    )(owners, *parts)


def middle_kernel(owns, received, left, right, block_out, grafted_out):
    size = left.shape[0]
    plain = jnp.where(owns[0] > 0, received[...], jnp.zeros_like(received))
    block_out[...] = plain
    block = plain.astype(jnp.float32)
    half = jnp.dot(left[...], plain, preferred_element_type=jnp.float32).astype(jnp.bfloat16)
    shaped = jnp.dot(half, right[...], preferred_element_type=jnp.float32)
    scale = 1.0 / (size * size)
    ratio = jnp.sqrt(jnp.sum(block * block, keepdims=True) * scale + graft_eps) / jnp.sqrt(
        jnp.sum(shaped * shaped, keepdims=True) * scale + graft_eps
    )
    grafted = shaped * ratio
    z_count = grafted_out.shape[0] // 4
    for z in range(z_count):
        for y in range(4):
            begin = (z * 4 + y) * rows
            grafted_out[y * z_count + z] = grafted[begin : begin + rows].astype(jnp.bfloat16)


def middle(owns, received, left, right):
    size = left.shape[0]
    vmem = pl.BlockSpec(memory_space=pltpu.VMEM)
    return pl.pallas_call(
        middle_kernel,
        out_shape=(
            jax.ShapeDtypeStruct((size, size), jnp.bfloat16),
            jax.ShapeDtypeStruct((size // rows, rows, size), jnp.bfloat16),
        ),
        in_specs=[pl.BlockSpec(memory_space=pltpu.SMEM)] + [vmem] * 3,
        out_specs=(vmem, vmem),
        compiler_params=pltpu.CompilerParams(vmem_limit_bytes=32 * 1024 * 1024),
        cost_estimate=pl.CostEstimate(
            flops=4 * size * size * size, bytes_accessed=10 * size * size, transcendentals=2
        ),
    )(owns, received, left, right)


def per_device(grad_partial, block_order, owner_slot, left_root, right_root):
    shard_count = lax.axis_size("z") * lax.axis_size("y")
    block_size = left_root.shape[2]
    group_size = grad_partial.shape[1] // (2 * lax.axis_size("x"))

    partial = grad_partial[0].reshape(-1, rows, block_size)
    sent, kept = place(block_order, partial)
    owners = lax.dynamic_slice_in_dim(owner_slot, first_of_group(group_size), group_size)
    owns = jnp.any(owners == lax.axis_index(("z", "y"))).astype(jnp.int32)[None]
    kept, owns = lax.optimization_barrier((kept, owns))
    chip = kept + swap_core(sent)

    def chip_sums(counts):
        def exchange(chip):
            chip = chip.reshape(-1, group_size, rows, block_size)
            parts, begin = [], 0
            for count in counts:
                part = chip[:, begin : begin + count]
                parts.append(lax.all_to_all(part, "x", 0, 0, tiled=True))
                begin += count
            return slots(owner_slot, parts, shard_count)

        return exchange

    at_once, in_turn = chip_sums((group_size,)), chip_sums((2, group_size - 2))
    outgoing = lax.cond(lax.axis_index("core") == 1, at_once, in_turn, chip)
    received = lax.all_to_all(outgoing, ("z", "y"), 0, 0, tiled=True)
    block, grafted = middle(
        owns, received.reshape(block_size, block_size), left_root[0, 0], right_root[0, 0]
    )
    returned = lax.all_to_all(grafted, ("y", "z"), 0, 0, tiled=True)
    places = owners % 4 * (shard_count // 4) + owners // 4
    update = jnp.take(returned, places, axis=0, mode="clip").reshape(group_size, -1)
    left_stat = jnp.einsum("ab,cb->ac", block, block, preferred_element_type=jnp.float32)
    right_stat = jnp.einsum("ba,bc->ac", block, block, preferred_element_type=jnp.float32)
    return (left_stat[None, None] / block_size, right_stat[None, None] / block_size, update)


def solution(mesh):
    rep_count, shard_count = mesh.devices.shape
    split = Mesh(
        mesh.devices.reshape(rep_count // 2, 2, shard_count // 4, 4), ("x", "core", "z", "y")
    )
    return jax.shard_map(
        per_device,
        mesh=split,
        in_specs=(
            P(("x", "core"), None, ("z", "y")),
            P(),
            P(),
            P(("x", "core"), ("z", "y"), None, None),
            P(("x", "core"), ("z", "y"), None, None),
        ),
        out_specs=(
            P(("x", "core"), ("z", "y"), None, None),
            P(("x", "core"), ("z", "y"), None, None),
            P(("x", "core"), ("z", "y")),
        ),
        check_vma=False,
    )
```
